128 devices in a mesh: row: 8 (over y_lo, x), col: 16 (over z, y_hi, core).
Axes of the slice: x: 4, y: 4 (y_hi: 2, y_lo: 2; y = y_hi * 2 + y_lo), z: 4, core: 2. Of those that a mesh axis runs over, the one named last changes fastest.
Arguments:
- pair_rep: float32 [512, 512, 128], P('row', 'col'), may hold values from -24 to 24
- gain_start: float32 [128], replicated, may hold values from 0.5 to 1.5
- project_start: bfloat16 [128, 512], replicated, may hold values from -0.5 to 0.5
- gate_bias_start: float32 [128], replicated, may hold values from -1 to 2
- bias_start: bfloat16 [128, 4], replicated, may hold values from -18 to 18
- out_start: bfloat16 [128, 128], replicated, may hold values from -0.5 to 0.5
- gain_end: float32 [128], replicated, may hold values from 0.5 to 1.5
- project_end: bfloat16 [128, 512], replicated, may hold values from -0.5 to 0.5
- gate_bias_end: float32 [128], replicated, may hold values from -1 to 2
- bias_end: bfloat16 [128, 4], replicated, may hold values from -18 to 18
- out_end: bfloat16 [128, 128], replicated, may hold values from -0.5 to 0.5
Outputs:
- pair_out: float32 [512, 512, 128], P('row', 'col')
The draws below stay inside these ranges and needn't reach their ends.
All inputs are finite; a program needn't handle non-finite values.
Results may differ from the reference program's by a relative error of at most 0.011.
Values may be sent and summed in bfloat16 or wider, within the bound.
A program may use at most 128 MiB of HBM per device.

```python
import math
import jax
import jax.numpy as jnp
from jax import lax

C = 128
H = 4
DH = 32
RESIDUES = 512


def draw_pair_rep(key, part):
    key = jax.random.fold_in(key, 11)
    key_base, key_pos, key_chan = jax.random.split(key, 3)
    base = jnp.clip(jax.random.normal(key_base, (RESIDUES, RESIDUES, C), jnp.float32), -4.0, 4.0)
    position_scale = 0.3 * jnp.exp(jax.random.uniform(key_pos, (RESIDUES, RESIDUES, 1), jnp.float32, 0.0, math.log(10.0)))
    channel_scale = jnp.exp(jax.random.uniform(key_chan, (1, 1, C), jnp.float32, math.log(0.5), math.log(2.0)))
    return base * position_scale * channel_scale


def bias_matrix(key):
    base = jnp.clip(jax.random.normal(key, (C, H), jnp.float32), -3.0, 3.0)
    return (base * (2.0 / math.sqrt(C))).astype(jnp.bfloat16)


def draw_bias_start(key, part):
    key = jax.random.fold_in(key, 23)
    return bias_matrix(key)


def draw_bias_end(key, part):
    key = jax.random.fold_in(key, 37)
    return bias_matrix(key)


def bell_draw(stream_key, extent, scale, reach, kind=jnp.bfloat16):
    drawn = scale * jax.random.normal(stream_key, extent, jnp.float32)
    return jnp.clip(drawn, min=-reach, max=reach).astype(kind)


def setup_inputs(seed: int = 0) -> dict:
    key_of = jax.random.split(jax.random.key(seed), 12)
    pair_rep = draw_pair_rep(jax.random.fold_in(key_of[11], 71), 0)
    gain_start = jnp.clip(jax.random.uniform(key_of[1], (C,), jnp.float32, 0.5, 1.5), 0.5, 1.5)
    project_start = bell_draw(key_of[2], (C, 4 * H * DH), C ** -0.5, 0.5)
    gate_bias_start = jnp.clip(jax.random.uniform(key_of[3], (H * DH,), jnp.float32, -1.0, 2.0), -1.0, 2.0)
    bias_start = draw_bias_start(jax.random.fold_in(key_of[11], 71), 0)
    out_start = bell_draw(key_of[5], (H * DH, C), (H * DH) ** -0.5, 0.5)
    gain_end = jnp.clip(jax.random.uniform(key_of[6], (C,), jnp.float32, 0.5, 1.5), 0.5, 1.5)
    project_end = bell_draw(key_of[7], (C, 4 * H * DH), C ** -0.5, 0.5)
    gate_bias_end = jnp.clip(jax.random.uniform(key_of[8], (H * DH,), jnp.float32, -1.0, 2.0), -1.0, 2.0)
    bias_end = draw_bias_end(jax.random.fold_in(key_of[11], 71), 0)
    out_end = bell_draw(key_of[10], (H * DH, C), (H * DH) ** -0.5, 0.5)
    return {"pair_rep": pair_rep, "gain_start": gain_start, "project_start": project_start, "gate_bias_start": gate_bias_start, "bias_start": bias_start, "out_start": out_start, "gain_end": gain_end, "project_end": project_end, "gate_bias_end": gate_bias_end, "bias_end": bias_end, "out_end": out_end}


def layer_norm(values, gain):
    centre_mean = lax.optimization_barrier(jnp.mean(values, axis=-1, keepdims=True))
    centred = values - centre_mean
    variance = lax.optimization_barrier(jnp.mean(centred * centred, axis=-1, keepdims=True))
    return (centred * lax.rsqrt(variance + 1e-05) * gain).astype(jnp.bfloat16)

def starting_update(pair_rep, gain, project, gate_bias, bias_weight, out_weight):
    residue_count = pair_rep.shape[0]
    inner_width = H * DH
    normed = layer_norm(pair_rep, gain)
    bias_full = jnp.dot(normed.reshape(-1, C), bias_weight, preferred_element_type=jnp.float32)
    bias_heads = jnp.transpose(bias_full.reshape(residue_count, residue_count, H), (2, 0, 1))
    row_blocks = normed.reshape(residue_count // 8, 8, residue_count, C)

    def one_block(block_rows):
        projected = jnp.dot(block_rows.reshape(-1, C), project, preferred_element_type=jnp.float32)
        projected = projected.reshape(8, residue_count, 4, H, DH)
        query_rows = projected[:, :, 0].astype(jnp.bfloat16)
        key_rows = projected[:, :, 1].astype(jnp.bfloat16)
        value_rows = projected[:, :, 2].astype(jnp.bfloat16)
        gate_open = jax.nn.sigmoid(projected[:, :, 3] + gate_bias.reshape(H, DH))
        scores = jnp.einsum('ijhd,ikhd->ihjk', query_rows.astype(jnp.float32), key_rows.astype(jnp.float32))
        scores = scores * DH ** (-0.5) + bias_heads[None]
        highest = lax.optimization_barrier(jnp.max(scores, axis=-1, keepdims=True))
        weights_exp = jnp.exp(scores - highest)
        normaliser = lax.optimization_barrier(jnp.sum(weights_exp, axis=-1))
        rounded = weights_exp.astype(jnp.bfloat16).astype(jnp.float32)
        attended = jnp.einsum('ihjk,ikhd->ijhd', rounded, value_rows.astype(jnp.float32))
        attended = attended / jnp.transpose(normaliser, (0, 2, 1))[..., None]
        gated = (gate_open * attended).astype(jnp.bfloat16).reshape(-1, inner_width)
        return jnp.dot(gated, out_weight, preferred_element_type=jnp.float32).reshape(8, residue_count, C)
    return lax.map(one_block, row_blocks).reshape(residue_count, residue_count, C)

def reference(pair_rep, gain_start, project_start, gate_bias_start, bias_start, out_start, gain_end, project_end, gate_bias_end, bias_end, out_end):
    first = pair_rep + starting_update(pair_rep, gain_start, project_start, gate_bias_start, bias_start, out_start)
    flipped = jnp.transpose(first, (1, 0, 2))
    update = starting_update(flipped, gain_end, project_end, gate_bias_end, bias_end, out_end)
    return first + jnp.transpose(update, (1, 0, 2))
```

```python
import functools

import jax
import jax.numpy as jnp
from jax import lax
from jax.experimental import pallas as pl
from jax.experimental.pallas import tpu as pltpu
from jax.sharding import PartitionSpec as P

MESH = pl.DeviceIdType.MESH
LOG2E = 1.4426950408889634
BF16 = jnp.bfloat16
F32 = jnp.float32


def layer_norm(values, gain):
    centred = values - jnp.mean(values, axis=-1, keepdims=True)
    variance = jnp.mean(centred * centred, axis=-1, keepdims=True)
    return (centred * lax.rsqrt(variance + 1e-05) * gain).astype(BF16)


def head_max(values):
    turned = values.T
    rows = turned.shape[1]
    turned = jnp.max(turned.reshape(4, 32, rows), axis=1, keepdims=True)
    return jnp.broadcast_to(turned, (4, 32, rows)).reshape(128, rows).T


def spread_weight(weight):
    head = lax.broadcasted_iota(jnp.int32, (128, 128), 1) // 32
    weight = weight.astype(F32)
    out = jnp.zeros((128, 128), F32)
    for h in range(4):
        out = jnp.where(head == h, weight[:, h : h + 1], out)
    return out.astype(BF16)


def bias_rows(normed, weight, rows):
    every = jnp.dot(normed, weight, preferred_element_type=F32) * LOG2E
    k_lane = lax.broadcasted_iota(jnp.int32, (1, 32, 128), 2) % 32
    k_row = lax.broadcasted_iota(jnp.int32, (1, 32, 128), 1)
    return jnp.sum(jnp.where(k_lane == k_row, every.reshape(rows, 32, 128), 0.0), axis=1)


def prepare(index, x, project, gate_bias, query, key, value, gate):
    projected = jnp.dot(x, project, preferred_element_type=F32)
    query[index] = (projected[:, :128] * (32**-0.5 * LOG2E)).astype(BF16)
    gate[index] = jax.nn.sigmoid(projected[:, 384:] + gate_bias)
    keys = projected[:, 128:256].astype(BF16).reshape(16, 32, 128)
    values = projected[:, 256:384].astype(BF16).reshape(16, 32, 128)
    head = lax.broadcasted_iota(jnp.int32, (1, 32, 128), 2) // 32
    for h in range(4):
        key[index, :, h] = jnp.where(head == h, keys, jnp.zeros_like(keys))
        value[index, :, h, :, :128] = jnp.where(head == h, values, jnp.zeros_like(values))


def attend(index, start, bias, query, key, value, gate, out):
    scores = lax.dot_general(
        query[index, pl.ds(start, 128)],
        key[index].reshape(2048, 128),
        (((1,), (1,)), ((), ())),
        preferred_element_type=F32,
    )
    slot = start // 32
    parts = [
        scores[:, 128 * b : 128 * (b + 1)]
        + bias[pl.ds(slot, 4), b].reshape(128, 128).astype(F32)
        for b in range(16)
    ]
    high = head_max(functools.reduce(jnp.maximum, parts))
    expo = jnp.concatenate([jnp.exp2(part - high).astype(BF16) for part in parts], axis=1)
    both = jnp.dot(expo, value[index].reshape(2048, 256), preferred_element_type=F32)
    out[index, pl.ds(start, 128)] = (
        gate[index, pl.ds(start, 128)] * (both[:, :128] / both[:, 128:])
    ).astype(BF16)


def remote(src, dst, send, recv, device):
    return pltpu.make_async_remote_copy(
        src_ref=src, dst_ref=dst, send_sem=send, recv_sem=recv, device_id=device, device_id_type=MESH
    )


def kernel(
    pair, gain_s, project_s, gate_bias_s, bias_s, out_s, gain_e, project_e, gate_bias_e, bias_e, out_e,
    result,
    normed_s, normed_e, mine_s, mine_e, line_s, line_e, whole_s, whole_e, full_s, full_e,
    query, key, value, gate, gated_s, gated_e, home_s, home_e, first,
    send_x_s, recv_x_s, send_x_e, recv_x_e, send_l_s, recv_l_s, send_l_e, recv_l_e,
    send_b_s, recv_b_s, send_b_e, recv_b_e, send_c_s, recv_c_s, send_c_e, recv_c_e,
    send_h_s, recv_h_s, send_h_e, recv_h_e,
):
    r = lax.axis_index("row")
    c = lax.axis_index("col")
    core = c % 2
    sibling = {"col": c + 1 - 2 * core}

    barrier = pltpu.get_barrier_semaphore()
    for s in range(1, 16):
        pl.semaphore_signal(barrier, inc=1, device_id={"col": (c + s) % 16}, device_id_type=MESH)
    for s in range(1, 8):
        pl.semaphore_signal(barrier, inc=1, device_id={"row": (r + s) % 8}, device_id_type=MESH)

    head = lax.broadcasted_iota(jnp.int32, (1, 32, 128), 2) // 32
    for i in range(4):
        for h in range(4):
            value[i, :, h, :, 128:] = jnp.broadcast_to(
                jnp.where(head == h, 1.0, 0.0).astype(BF16), (16, 32, 128)
            )


    def share_bias(place, slot, device_of, line, full, send_b, recv_b, send_c):
        values = line[...]
        high = head_max(jnp.max(values, axis=0))
        full[slot] = (values - high[None]).astype(BF16)
        mate = place + 1 - 2 * (place % 2)
        order = [mate]
        for t in range(1, 4):
            part = (place // 2 + 4 - t) % 4
            order += [2 * part, 2 * part + 1]
        for other in order:
            remote(
                full.at[slot], full.at[slot], send_b.at[other], recv_b.at[place], device_of(other)
            ).start()

    def attention(place, device_of, x, project, gate_bias, full, gated, send_b, recv_b, send_c, recv_c, send_home):
        def copy_to_sibling(other):
            spot = 2 * other + core
            return remote(full.at[spot], full.at[spot], send_c.at[other], recv_c.at[other], sibling)

        def from_sibling(other):
            spot = 2 * other + 1 - core
            return remote(full.at[spot], full.at[spot], send_c.at[other], recv_c.at[other], sibling)

        copy_to_sibling(place).start()

        def one_row(i, carry):
            prepare(i, x[i], project[...], gate_bias[...], query, key, value, gate)
            return carry

        lax.fori_loop(0, 4, one_row, 0)

        def chunk(t, carry):
            part = (place // 2 + t) % 4
            for u in range(2):
                other = 2 * part + u

                @pl.when(other != place)
                def _():
                    spot = 2 * other + core
                    remote(
                        full.at[spot], full.at[spot], send_b.at[other], recv_b.at[other], device_of(other)
                    ).wait_recv()
                    copy_to_sibling(other).start()

            for u in range(2):
                from_sibling(2 * part + u).wait_recv()
            start = pl.multiple_of(part * 128, 128)
            for i in range(4):
                attend(i, start, full, query, key, value, gate, gated)
            send_home(part)
            return carry

        lax.fori_loop(0, 4, chunk, 0)
        for other in range(8):
            copy_to_sibling(other).wait_send()

    weight = spread_weight(bias_s[...])

    def norm_start(t, carry):
        normed = layer_norm(pair[pl.ds(pl.multiple_of(t * 256, 256), 256)], gain_s[...])
        normed_s[pl.ds(t * 8, 8)] = normed.reshape(8, 32, 128)
        mine_s[pl.ds(pl.multiple_of(t * 8, 8), 8)] = bias_rows(normed, weight, 8)
        return carry

    lax.fori_loop(0, 8, norm_start, 0)

    pl.semaphore_wait(barrier, 22)

    def line_copy_s(s):
        p = (c + s) % 16
        return remote(
            mine_s.at[pl.ds(pl.multiple_of(32 * (p % 2), 32), 32)], line_s.at[c],
            send_l_s.at[s], recv_l_s.at[s], {"col": p},
        )

    def tile_copy_s(s):
        p = (c + s) % 16
        return remote(
            normed_s.at[pl.ds(4 * p, 4)], whole_s.at[:, pl.ds(pl.multiple_of(32 * c, 32), 32)],
            send_x_s.at[s], recv_x_s.at[s], {"col": p},
        )

    for s in range(1, 16):
        line_copy_s(s).start()
    for s in range(1, 16):
        tile_copy_s(s).start()
    line_s[c] = mine_s[pl.ds(pl.multiple_of(32 * core, 32), 32)]
    whole_s[:, pl.ds(pl.multiple_of(32 * c, 32), 32)] = normed_s[pl.ds(4 * c, 4)]
    for s in range(1, 16):
        line_copy_s(s).wait_recv()
    share_bias(r, 2 * r + core, lambda other: {"row": other}, line_s, full_s, send_b_s, recv_b_s, send_c_s)
    for s in range(1, 16):
        tile_copy_s(s).wait_recv()

    def home_copy_s(p):
        return remote(
            gated_s.at[:, pl.ds(pl.multiple_of(32 * p, 32), 32)], home_s.at[pl.ds(4 * c, 4)],
            send_h_s.at[p], recv_h_s.at[c], {"col": p},
        )

    def send_home_s(part):
        for u in range(4):
            p = 4 * part + u

            @pl.when(p != c)
            def _():
                home_copy_s(p).start()

            @pl.when(p == c)
            def _():
                home_s[pl.ds(4 * c, 4)] = gated_s[:, pl.ds(pl.multiple_of(32 * c, 32), 32)]

    attention(
        r, lambda other: {"row": other}, whole_s, project_s, gate_bias_s, full_s, gated_s,
        send_b_s, recv_b_s, send_c_s, recv_c_s, send_home_s,
    )
    for s in range(1, 16):
        p = (c + s) % 16
        remote(
            gated_s.at[:, pl.ds(0, 32)], home_s.at[pl.ds(4 * p, 4)], send_h_s.at[p], recv_h_s.at[p], {"col": p}
        ).wait_recv()

    weight_e = spread_weight(bias_e[...])

    def residual(t, carry):
        rows = pl.ds(pl.multiple_of(t * 256, 256), 256)
        update = jnp.dot(
            home_s[pl.ds(t * 8, 8)].reshape(256, 128), out_s[...], preferred_element_type=F32
        )
        first[rows] = pair[rows] + update
        return carry

    lax.fori_loop(0, 8, residual, 0)

    def norm_end(t, carry):
        values = jnp.concatenate([first[pl.ds(t * 8 + u, 64, stride=32)] for u in range(8)], axis=0)
        normed = layer_norm(values, gain_e[...])
        normed_e[pl.ds(t * 8, 8)] = normed.reshape(8, 64, 128)
        rows = bias_rows(normed, weight_e, 16).reshape(8, 2, 128)
        for b in range(2):
            mine_e[b, pl.ds(pl.multiple_of(t * 8, 8), 8)] = rows[:, b]
        return carry

    lax.fori_loop(0, 4, norm_end, 0)

    def line_copy_e(s):
        p = (r + s) % 8
        return remote(mine_e, line_e.at[pl.ds(2 * r, 2)], send_l_e.at[s], recv_l_e.at[s], {"row": p})

    def tile_copy_e(s):
        p = (r + s) % 8
        return remote(
            normed_e.at[pl.ds(4 * p, 4)], whole_e.at[:, pl.ds(pl.multiple_of(64 * r, 64), 64)],
            send_x_e.at[s], recv_x_e.at[s], {"row": p},
        )

    for s in range(1, 8):
        line_copy_e(s).start()
    for s in range(1, 8):
        tile_copy_e(s).start()
    line_e[pl.ds(2 * r, 2)] = mine_e[...]
    whole_e[:, pl.ds(pl.multiple_of(64 * r, 64), 64)] = normed_e[pl.ds(4 * r, 4)]
    for s in range(1, 8):
        line_copy_e(s).wait_recv()
    share_bias(c // 2, c, lambda other: {"col": 2 * other + core}, line_e, full_e, send_b_e, recv_b_e, send_c_e)
    for s in range(1, 8):
        tile_copy_e(s).wait_recv()

    def home_copy_e(p):
        return remote(
            gated_e.at[:, pl.ds(pl.multiple_of(64 * p, 64), 64)], home_e.at[pl.ds(4 * r, 4)],
            send_h_e.at[p], recv_h_e.at[r], {"row": p},
        )

    def send_home_e(part):
        for u in range(2):
            p = 2 * part + u

            @pl.when(p != r)
            def _():
                home_copy_e(p).start()

            @pl.when(p == r)
            def _():
                home_e[pl.ds(4 * r, 4)] = gated_e[:, pl.ds(pl.multiple_of(64 * r, 64), 64)]

    attention(
        c // 2, lambda other: {"col": 2 * other + core}, whole_e, project_e, gate_bias_e, full_e, gated_e,
        send_b_e, recv_b_e, send_c_e, recv_c_e, send_home_e,
    )
    for s in range(1, 8):
        p = (r + s) % 8
        remote(
            gated_e.at[:, pl.ds(0, 64)], home_e.at[pl.ds(4 * p, 4)], send_h_e.at[p], recv_h_e.at[p], {"row": p}
        ).wait_recv()

    def finish(t, carry):
        update = jnp.dot(
            home_e[pl.ds(t * 8, 8)].reshape(512, 128), out_e[...], preferred_element_type=F32
        )
        for u in range(8):
            rows = pl.ds(t * 8 + u, 64, stride=32)
            result[rows] = first[rows] + update[64 * u : 64 * (u + 1)]
        return carry

    lax.fori_loop(0, 4, finish, 0)

    for s in range(1, 16):
        line_copy_s(s).wait_send()
        tile_copy_s(s).wait_send()
        home_copy_s((c + s) % 16).wait_send()
    for s in range(1, 8):
        line_copy_e(s).wait_send()
        tile_copy_e(s).wait_send()
        home_copy_e((r + s) % 8).wait_send()
        other = (r + s) % 8
        remote(
            full_s.at[2 * r + core], full_s.at[2 * r + core], send_b_s.at[other], recv_b_s.at[other], {"row": other}
        ).wait_send()
        other = (c // 2 + s) % 8
        remote(
            full_e.at[c], full_e.at[c], send_b_e.at[other], recv_b_e.at[other], {"col": 2 * other + core}
        ).wait_send()


def local(pair, gain_s, project_s, gate_bias_s, bias_s, out_s, gain_e, project_e, gate_bias_e, bias_e, out_e):
    vmem = pl.BlockSpec(memory_space=pltpu.VMEM)
    dma = pltpu.SemaphoreType.DMA
    out = pl.pallas_call(
        kernel,
        out_shape=jax.ShapeDtypeStruct((2048, 128), F32),
        in_specs=[vmem] * 11,
        out_specs=vmem,
        scratch_shapes=[
            pltpu.VMEM((64, 32, 128), BF16),
            pltpu.VMEM((32, 64, 128), BF16),
            pltpu.VMEM((64, 128), F32),
            pltpu.VMEM((2, 32, 128), F32),
            pltpu.VMEM((16, 32, 128), F32),
            pltpu.VMEM((16, 32, 128), F32),
            pltpu.VMEM((4, 512, 128), BF16),
            pltpu.VMEM((4, 512, 128), BF16),
            pltpu.VMEM((16, 16, 32, 128), BF16),
            pltpu.VMEM((16, 16, 32, 128), BF16),
            pltpu.VMEM((4, 512, 128), BF16),
            pltpu.VMEM((4, 16, 4, 32, 128), BF16),
            pltpu.VMEM((4, 16, 4, 32, 256), BF16),
            pltpu.VMEM((4, 512, 128), F32),
            pltpu.VMEM((4, 512, 128), BF16),
            pltpu.VMEM((4, 512, 128), BF16),
            pltpu.VMEM((64, 32, 128), BF16),
            pltpu.VMEM((32, 64, 128), BF16),
            pltpu.VMEM((2048, 128), F32),
        ]
        + [dma((n,)) for n in (16, 16, 8, 8) * 2 + (8,) * 8 + (16, 16, 8, 8)],
        compiler_params=pltpu.CompilerParams(
            collective_id=0, has_side_effects=True, vmem_limit_bytes=56 * 2**20
        ),
    )(
        pair.reshape(2048, 128),
        gain_s.reshape(1, 128), project_s, gate_bias_s.reshape(1, 128), bias_s, out_s,
        gain_e.reshape(1, 128), project_e, gate_bias_e.reshape(1, 128), bias_e, out_e,
    )
    return out.reshape(pair.shape)


def solution(mesh):
    return jax.shard_map(
        local,
        mesh=mesh,
        in_specs=(P("row", "col", None), P(), P(), P(), P(), P(), P(), P(), P(), P(), P()),
        out_specs=P("row", "col", None),
        check_vma=False,
    )
```

```python
import functools

import jax
import jax.numpy as jnp
from jax import lax
from jax.experimental import pallas as pl
from jax.experimental.pallas import tpu as pltpu
from jax.sharding import PartitionSpec as P

MESH = pl.DeviceIdType.MESH
LOG2E = 1.4426950408889634
BF16 = jnp.bfloat16
F32 = jnp.float32


def layer_norm(values, gain):
    centred = values - jnp.mean(values, axis=-1, keepdims=True)
    variance = jnp.mean(centred * centred, axis=-1, keepdims=True)
    return (centred * lax.rsqrt(variance + 1e-05) * gain).astype(BF16)


def head_max(values):
    turned = values.T
    rows = turned.shape[1]
    turned = jnp.max(turned.reshape(4, 32, rows), axis=1, keepdims=True)
    return jnp.broadcast_to(turned, (4, 32, rows)).reshape(128, rows).T


def spread_weight(weight):
    head = lax.broadcasted_iota(jnp.int32, (128, 128), 0) // 32
    weight = weight.astype(F32)
    out = jnp.zeros((128, 128), F32)
    for h in range(4):
        out = jnp.where(head == h, weight[h : h + 1], out)
    return out.astype(BF16)


def bias_all(normed, weight):
    dims = (((1,), (1,)), ((), ()))
    return lax.dot_general(normed, weight, dims, preferred_element_type=F32) * LOG2E


def bias_rows(normed, weight, rows):
    every = bias_all(normed, weight)
    k_lane = lax.broadcasted_iota(jnp.int32, (1, 32, 128), 2) % 32
    k_row = lax.broadcasted_iota(jnp.int32, (1, 32, 128), 1)
    return jnp.sum(jnp.where(k_lane == k_row, every.reshape(rows, 32, 128), 0.0), axis=1)


def prepare(index, x, project, gate_bias, query, key, value, gate):
    projected = jnp.dot(x, project, preferred_element_type=F32)
    query[index] = (projected[:, :128] * (32**-0.5 * LOG2E)).astype(BF16)
    gate[index] = jax.nn.sigmoid(projected[:, 384:] + gate_bias)
    keys = projected[:, 128:256].astype(BF16).reshape(16, 32, 128)
    values = projected[:, 256:384].astype(BF16).reshape(16, 32, 128)
    head = lax.broadcasted_iota(jnp.int32, (1, 32, 128), 2) // 32
    for h in range(4):
        key[index, :, h] = jnp.where(head == h, keys, jnp.zeros_like(keys))
        value[index, :, h, :, :128] = jnp.where(head == h, values, jnp.zeros_like(values))


def attend(index, start, bias, query, key, value, gate, out):
    scores = lax.dot_general(
        query[index, pl.ds(start, 128)],
        key[index].reshape(2048, 128),
        (((1,), (1,)), ((), ())),
        preferred_element_type=F32,
    )
    slot = start // 32
    parts = [
        scores[:, 128 * b : 128 * (b + 1)]
        + bias[pl.ds(slot, 4), b].reshape(128, 128).astype(F32)
        for b in range(16)
    ]
    high = head_max(functools.reduce(jnp.maximum, parts))
    expo = jnp.concatenate([jnp.exp2(part - high).astype(BF16) for part in parts], axis=1)
    both = jnp.dot(expo, value[index].reshape(2048, 256), preferred_element_type=F32)
    out[index, pl.ds(start, 128)] = (
        gate[index, pl.ds(start, 128)] * (both[:, :128] / both[:, 128:])
    ).astype(BF16)


def shift_bias(line, full, slot):
    values = line[...]
    full[slot] = (values - head_max(jnp.max(values, axis=0))[None]).astype(BF16)


def remote(src, dst, send, recv, device):
    return pltpu.make_async_remote_copy(
        src_ref=src, dst_ref=dst, send_sem=send, recv_sem=recv, device_id=device, device_id_type=MESH
    )


def kernel(
    pair, gain_s, project_s, gate_bias_s, bias_s, out_s, gain_e, project_e, gate_bias_e, bias_e, out_e,
    result,
    normed_s, normed_e, mine_s, mine_e, line_s, line_e, whole_s, whole_e, full_s, full_e,
    query, key, value, gate, gated_s, gated_e, home_s, home_e, first, swap,
    send_x_s, recv_x_s, send_x_e, recv_x_e, send_l_s, recv_l_s, send_l_e, recv_l_e,
    send_b_s, recv_b_s, send_b_e, recv_b_e, send_c_s, recv_c_s, send_c_e, recv_c_e,
    send_h_s, recv_h_s, send_h_e, recv_h_e,
):
    r = lax.axis_index("row")
    c = lax.axis_index("col")
    core = c % 2
    sibling = {"col": c + 1 - 2 * core}

    barrier = pltpu.get_barrier_semaphore()
    for s in range(1, 16):
        pl.semaphore_signal(barrier, inc=1, device_id={"col": (c + s) % 16}, device_id_type=MESH)
    for s in range(1, 8):
        pl.semaphore_signal(barrier, inc=1, device_id={"row": (r + s) % 8}, device_id_type=MESH)

    mine_e[...] = jnp.zeros_like(mine_e)
    head = lax.broadcasted_iota(jnp.int32, (1, 32, 128), 2) // 32
    for i in range(4):
        for h in range(4):
            value[i, :, h, :, 128:] = jnp.broadcast_to(
                jnp.where(head == h, 1.0, 0.0).astype(BF16), (16, 32, 128)
            )


    def turn(t, lane):
        return 0 if t == 0 else 1 + (t - 1 + lane) % 3

    def send_bias(t, place, lane, slot, device_of, full, send_b, recv_b):
        if t == 0:
            others = [place + 1 - 2 * (place % 2)]
        else:
            part = (place // 2 + 4 - turn(t, lane)) % 4
            others = [2 * part, 2 * part + 1]
        for other in others:
            remote(
                full.at[slot], full.at[slot], send_b.at[other], recv_b.at[place], device_of(other)
            ).start()

    def attention(place, lane, device_of, x, project, gate_bias, full, gated, send_b, recv_b, send_c, recv_c, send_home, ready):
        def copy_to_sibling(other):
            spot = 2 * other + core
            return remote(full.at[spot], full.at[spot], send_c.at[other], recv_c.at[other], sibling)

        def from_sibling(other):
            spot = 2 * other + 1 - core
            return remote(full.at[spot], full.at[spot], send_c.at[other], recv_c.at[other], sibling)

        def pass_on(other):
            spot = 2 * other + core
            remote(
                full.at[spot], full.at[spot], send_b.at[other], recv_b.at[other], device_of(other)
            ).wait_recv()
            copy_to_sibling(other).start()

        copy_to_sibling(place).start()
        ready()

        def one_row(i, carry):
            prepare(i, x[i], project[...], gate_bias[...], query, key, value, gate)
            return carry

        lax.fori_loop(0, 4, one_row, 0)
        pass_on(place + 1 - 2 * (place % 2))

        def chunk(t, carry):
            step = 1 - (3 - t) // 3
            part = (place // 2 + step * (1 + (t + 2 + lane) % 3)) % 4
            after = (place // 2 + 1 + (t + lane) % 3) % 4
            for u in range(2):
                from_sibling(2 * part + u).wait_recv()

            @pl.when(t < 3)
            def _():
                for u in range(2):
                    pass_on(2 * after + u)

            start = pl.multiple_of(part * 128, 128)
            for i in range(4):
                attend(i, start, full, query, key, value, gate, gated)
            send_home(part)
            return carry

        lax.fori_loop(0, 4, chunk, 0)
        for other in range(8):
            copy_to_sibling(other).wait_send()

    weight = spread_weight(bias_s[...])

    def norm_start(t, carry):
        normed = layer_norm(pair[pl.ds(pl.multiple_of(t * 256, 256), 256)], gain_s[...])
        normed_s[pl.ds(t * 8, 8)] = normed.reshape(8, 32, 128)
        mine_s[pl.ds(pl.multiple_of(t * 8, 8), 8)] = bias_rows(normed, weight, 8)
        return carry

    lax.fori_loop(0, 8, norm_start, 0)

    pl.semaphore_wait(barrier, 22)

    def line_copy_s(s):
        p = (c + s) % 16
        return remote(
            mine_s.at[pl.ds(pl.multiple_of(32 * (p % 2), 32), 32)], line_s.at[c],
            send_l_s.at[s], recv_l_s.at[s], {"col": p},
        )

    def tile_copy_s(s):
        p = (c + s) % 16
        return remote(
            normed_s.at[pl.ds(4 * p, 4)], whole_s.at[:, pl.ds(pl.multiple_of(32 * c, 32), 32)],
            send_x_s.at[s], recv_x_s.at[s], {"col": p},
        )

    for s in range(1, 16):
        line_copy_s(s).start()
    for s in range(1, 16):
        tile_copy_s(s).start()
    line_s[c] = mine_s[pl.ds(pl.multiple_of(32 * core, 32), 32)]
    whole_s[:, pl.ds(pl.multiple_of(32 * c, 32), 32)] = normed_s[pl.ds(4 * c, 4)]
    for s in range(1, 16):
        line_copy_s(s).wait_recv()
    shift_bias(line_s, full_s, 2 * r + core)
    for t in range(4):
        send_bias(t, r, c // 4, 2 * r + core, lambda other: {"row": other}, full_s, send_b_s, recv_b_s)

    def ready_s():
        for s in range(1, 16):
            tile_copy_s(s).wait_recv()

    def home_copy_s(p):
        return remote(
            gated_s.at[:, pl.ds(pl.multiple_of(32 * p, 32), 32)], home_s.at[pl.ds(4 * c, 4)],
            send_h_s.at[p], recv_h_s.at[c], {"col": p},
        )

    def send_home_s(part):
        for u in range(4):
            p = 4 * part + u

            @pl.when(p != c)
            def _():
                home_copy_s(p).start()

            @pl.when(p == c)
            def _():
                home_s[pl.ds(4 * c, 4)] = gated_s[:, pl.ds(pl.multiple_of(32 * c, 32), 32)]

    attention(
        r, c // 4, lambda other: {"row": other}, whole_s, project_s, gate_bias_s, full_s, gated_s,
        send_b_s, recv_b_s, send_c_s, recv_c_s, send_home_s, ready_s,
    )

    weight_e = spread_weight(bias_e[...])
    late_s = (c // 4 + 4 - r // 2) % 4
    lane = lax.broadcasted_iota(jnp.int32, (32, 128), 1) % 32

    def residual(e, carry):
        part = (e // 3) * 3 + (1 - e // 3) * ((late_s + 5 - e) % 3)
        for u in range(4):
            p = 4 * part + u

            @pl.when(p != c)
            def _():
                remote(
                    gated_s.at[:, pl.ds(0, 32)], home_s.at[pl.ds(4 * p, 4)],
                    send_h_s.at[p], recv_h_s.at[p], {"col": p},
                ).wait_recv()

        rows = pl.ds(pl.multiple_of(part * 512, 512), 512)
        update = jnp.dot(
            home_s[pl.ds(part * 16, 16)].reshape(512, 128), out_s[...], preferred_element_type=F32
        )
        total = pair[rows] + update
        first[rows] = total
        normed = layer_norm(total, gain_e[...])
        swap[rows] = normed.astype(F32)
        every = bias_all(normed, weight_e).reshape(16, 32, 128)
        here = lane - 16 * (part % 2)
        mixed = mine_e[part // 2]
        for u in range(16):
            mixed = jnp.where(here == u, every[u], mixed)
        mine_e[part // 2] = mixed
        return carry

    lax.fori_loop(0, 4, residual, 0)

    def line_copy_e(s):
        p = (r + s) % 8
        return remote(mine_e, line_e.at[pl.ds(2 * r, 2)], send_l_e.at[s], recv_l_e.at[s], {"row": p})

    def tile_copy_e(s):
        p = (r + s) % 8
        return remote(
            normed_e.at[pl.ds(4 * p, 4)], whole_e.at[:, pl.ds(pl.multiple_of(64 * r, 64), 64)],
            send_x_e.at[s], recv_x_e.at[s], {"row": p},
        )

    for s in range(1, 8):
        line_copy_e(s).start()

    def turned(t, carry):
        for u in range(8):
            normed_e[t * 8 + u] = swap[pl.ds(t * 8 + u, 64, stride=32)].astype(BF16)
        return carry

    lax.fori_loop(0, 4, turned, 0)
    for s in range(1, 8):
        tile_copy_e(s).start()
    line_e[pl.ds(2 * r, 2)] = mine_e[...]
    whole_e[:, pl.ds(pl.multiple_of(64 * r, 64), 64)] = normed_e[pl.ds(4 * r, 4)]
    for s in range(1, 8):
        line_copy_e(s).wait_recv()
    shift_bias(line_e, full_e, c)
    for t in range(4):
        send_bias(t, c // 2, r // 2, c, lambda other: {"col": 2 * other + core}, full_e, send_b_e, recv_b_e)

    def ready_e():
        for s in range(1, 8):
            tile_copy_e(s).wait_recv()

    def home_copy_e(p):
        return remote(
            gated_e.at[:, pl.ds(pl.multiple_of(64 * p, 64), 64)], home_e.at[pl.ds(4 * r, 4)],
            send_h_e.at[p], recv_h_e.at[r], {"row": p},
        )

    def send_home_e(part):
        for u in range(2):
            p = 2 * part + u

            @pl.when(p != r)
            def _():
                home_copy_e(p).start()

            @pl.when(p == r)
            def _():
                home_e[pl.ds(4 * r, 4)] = gated_e[:, pl.ds(pl.multiple_of(64 * r, 64), 64)]

    attention(
        c // 2, r // 2, lambda other: {"col": 2 * other + core}, whole_e, project_e, gate_bias_e, full_e, gated_e,
        send_b_e, recv_b_e, send_c_e, recv_c_e, send_home_e, ready_e,
    )
    late_e = (r // 2 + 4 - c // 4) % 4

    def finish(e, carry):
        part = (e // 3) * 3 + (1 - e // 3) * ((late_e + 5 - e) % 3)
        for u in range(2):
            p = 2 * part + u

            @pl.when(p != r)
            def _():
                remote(
                    gated_e.at[:, pl.ds(0, 64)], home_e.at[pl.ds(4 * p, 4)],
                    send_h_e.at[p], recv_h_e.at[p], {"row": p},
                ).wait_recv()

        update = jnp.dot(
            home_e[pl.ds(part * 8, 8)].reshape(512, 128), out_e[...], preferred_element_type=F32
        )
        for u in range(8):
            rows = pl.ds(part * 8 + u, 64, stride=32)
            result[rows] = first[rows] + update[64 * u : 64 * (u + 1)]
        return carry

    lax.fori_loop(0, 4, finish, 0)

    for s in range(1, 16):
        line_copy_s(s).wait_send()
        tile_copy_s(s).wait_send()
        home_copy_s((c + s) % 16).wait_send()
    for s in range(1, 8):
        line_copy_e(s).wait_send()
        tile_copy_e(s).wait_send()
        home_copy_e((r + s) % 8).wait_send()
        other = (r + s) % 8
        remote(
            full_s.at[2 * r + core], full_s.at[2 * r + core], send_b_s.at[other], recv_b_s.at[other], {"row": other}
        ).wait_send()
        other = (c // 2 + s) % 8
        remote(
            full_e.at[c], full_e.at[c], send_b_e.at[other], recv_b_e.at[other], {"col": 2 * other + core}
        ).wait_send()


def local(pair, gain_s, project_s, gate_bias_s, bias_s, out_s, gain_e, project_e, gate_bias_e, bias_e, out_e):
    vmem = pl.BlockSpec(memory_space=pltpu.VMEM)
    dma = pltpu.SemaphoreType.DMA
    out = pl.pallas_call(
        kernel,
        out_shape=jax.ShapeDtypeStruct((2048, 128), F32),
        in_specs=[vmem] * 11,
        out_specs=vmem,
        scratch_shapes=[
            pltpu.VMEM((64, 32, 128), BF16),
            pltpu.VMEM((32, 64, 128), BF16),
            pltpu.VMEM((64, 128), F32),
            pltpu.VMEM((2, 32, 128), F32),
            pltpu.VMEM((16, 32, 128), F32),
            pltpu.VMEM((16, 32, 128), F32),
            pltpu.VMEM((4, 512, 128), BF16),
            pltpu.VMEM((4, 512, 128), BF16),
            pltpu.VMEM((16, 16, 32, 128), BF16),
            pltpu.VMEM((16, 16, 32, 128), BF16),
            pltpu.VMEM((4, 512, 128), BF16),
            pltpu.VMEM((4, 16, 4, 32, 128), BF16),
            pltpu.VMEM((4, 16, 4, 32, 256), BF16),
            pltpu.VMEM((4, 512, 128), F32),
            pltpu.VMEM((4, 512, 128), BF16),
            pltpu.VMEM((4, 512, 128), BF16),
            pltpu.VMEM((64, 32, 128), BF16),
            pltpu.VMEM((32, 64, 128), BF16),
            pltpu.VMEM((2048, 128), F32),
            pltpu.VMEM((2048, 128), F32),
        ]
        + [dma((n,)) for n in (16, 16, 8, 8) * 2 + (8,) * 8 + (16, 16, 8, 8)],
        compiler_params=pltpu.CompilerParams(
            collective_id=0, has_side_effects=True, vmem_limit_bytes=56 * 2**20
        ),
    )(
        pair.reshape(2048, 128),
        gain_s.reshape(1, 128), project_s, gate_bias_s.reshape(1, 128), bias_s.T, out_s,
        gain_e.reshape(1, 128), project_e, gate_bias_e.reshape(1, 128), bias_e.T, out_e,
    )
    return out.reshape(pair.shape)


def solution(mesh):
    return jax.shard_map(
        local,
        mesh=mesh,
        in_specs=(P("row", "col", None), P(), P(), P(), P(), P(), P(), P(), P(), P(), P()),
        out_specs=P("row", "col", None),
        check_vma=False,
    )
```

```python
import functools

import jax
import jax.numpy as jnp
from jax import lax
from jax.experimental import pallas as pl
from jax.experimental.pallas import tpu as pltpu
from jax.sharding import PartitionSpec as P

MESH = pl.DeviceIdType.MESH
LOG2E = 1.4426950408889634
BF16 = jnp.bfloat16
F32 = jnp.float32


def layer_norm(values, gain):
    centred = values - jnp.mean(values, axis=-1, keepdims=True)
    variance = jnp.mean(centred * centred, axis=-1, keepdims=True)
    return (centred * lax.rsqrt(variance + 1e-05) * gain).astype(BF16)


def head_max(values):
    turned = values.T
    rows = turned.shape[1]
    turned = jnp.max(turned.reshape(4, 32, rows), axis=1, keepdims=True)
    return jnp.broadcast_to(turned, (4, 32, rows)).reshape(128, rows).T


def spread_weight(weight):
    head = lax.broadcasted_iota(jnp.int32, (128, 128), 0) // 32
    weight = weight.astype(F32)
    out = jnp.zeros((128, 128), F32)
    for h in range(4):
        out = jnp.where(head == h, weight[h : h + 1], out)
    return out.astype(BF16)


def bias_all(normed, weight):
    dims = (((1,), (1,)), ((), ()))
    return lax.dot_general(normed, weight, dims, preferred_element_type=F32) * LOG2E


def bias_rows(normed, weight, rows):
    every = bias_all(normed, weight)
    k_lane = lax.broadcasted_iota(jnp.int32, (1, 32, 128), 2) % 32
    k_row = lax.broadcasted_iota(jnp.int32, (1, 32, 128), 1)
    return jnp.sum(jnp.where(k_lane == k_row, every.reshape(rows, 32, 128), 0.0), axis=1)


def prepare(index, x, project, gate_bias, query, key, value, gate):
    projected = jnp.dot(x, project, preferred_element_type=F32)
    query[index] = (projected[:, :128] * (32**-0.5 * LOG2E)).astype(BF16)
    gate[index] = jax.nn.sigmoid(projected[:, 384:] + gate_bias)
    keys = projected[:, 128:256].astype(BF16).reshape(16, 32, 128)
    values = projected[:, 256:384].astype(BF16).reshape(16, 32, 128)
    head = lax.broadcasted_iota(jnp.int32, (1, 32, 128), 2) // 32
    for h in range(4):
        key[index, :, h] = jnp.where(head == h, keys, jnp.zeros_like(keys))
        value[index, :, h, :, :128] = jnp.where(head == h, values, jnp.zeros_like(values))


def attend(index, pair, bias, query, key, value, gate, out):
    rows = [pl.ds(pl.multiple_of(64 * place, 64), 64) for place in pair]
    scores = lax.dot_general(
        jnp.concatenate([query[index, at] for at in rows], axis=0),
        key[index].reshape(2048, 128),
        (((1,), (1,)), ((), ())),
        preferred_element_type=F32,
    )
    parts = []
    for b in range(16):
        added = [bias[pl.ds(2 * place, 2), b].reshape(64, 128) for place in pair]
        parts.append(scores[:, 128 * b : 128 * (b + 1)] + jnp.concatenate(added, axis=0).astype(F32))
    high = head_max(functools.reduce(jnp.maximum, parts))
    expo = jnp.concatenate([jnp.exp2(part - high).astype(BF16) for part in parts], axis=1)
    both = jnp.dot(expo, value[index].reshape(2048, 256), preferred_element_type=F32)
    mean = both[:, :128] / both[:, 128:]
    for u, at in enumerate(rows):
        out[index, at] = (gate[index, at] * mean[64 * u : 64 * (u + 1)]).astype(BF16)


def shift_bias(line, full, slot):
    values = line[...]
    full[slot] = (values - head_max(jnp.max(values, axis=0))[None]).astype(BF16)


def remote(src, dst, send, recv, device):
    return pltpu.make_async_remote_copy(
        src_ref=src, dst_ref=dst, send_sem=send, recv_sem=recv, device_id=device, device_id_type=MESH
    )


def kernel(
    pair, gain_s, project_s, gate_bias_s, bias_s, out_s, gain_e, project_e, gate_bias_e, bias_e, out_e,
    result,
    normed_s, normed_e, mine_s, mine_e, line_s, line_e, whole_s, whole_e, full_s, full_e,
    query, key, value, gate, gated_s, gated_e, home_s, home_e, first, swap,
    send_x_s, recv_x_s, send_x_e, recv_x_e, send_l_s, recv_l_s, send_l_e, recv_l_e,
    send_b_s, recv_b_s, send_b_e, recv_b_e, send_c_s, recv_c_s, send_c_e, recv_c_e,
    send_h_s, recv_h_s, send_h_e, recv_h_e,
):
    r = lax.axis_index("row")
    c = lax.axis_index("col")
    core = c % 2
    sibling = {"col": c + 1 - 2 * core}
    x, y_lo = r % 4, r // 4
    z, y_hi = c // 4, (c // 2) % 2

    across = {"row": 4 * (1 - y_lo) + x, "col": 4 * z + 2 * (1 - y_hi) + core}
    above = {"row": 4 * (1 - y_lo) + x, "col": 4 * z + 2 * ((y_hi + y_lo) % 2) + core}

    barrier = pltpu.get_barrier_semaphore()
    for s in range(1, 16):
        pl.semaphore_signal(barrier, inc=1, device_id={"col": (c + s) % 16}, device_id_type=MESH)
    for s in range(1, 8):
        pl.semaphore_signal(barrier, inc=1, device_id={"row": (r + s) % 8}, device_id_type=MESH)
    pl.semaphore_signal(barrier, inc=1, device_id=across, device_id_type=MESH)

    mine_e[...] = jnp.zeros_like(mine_e)
    head = lax.broadcasted_iota(jnp.int32, (1, 32, 128), 2) // 32
    for i in range(4):
        for h in range(4):
            value[i, :, h, :, 128:] = jnp.broadcast_to(
                jnp.where(head == h, 1.0, 0.0).astype(BF16), (16, 32, 128)
            )


    def attention(ring, line, whole, project, gate_bias, full, gated, sems, ready, send_home):
        a, b, lane, index, device_of, mate = ring
        send_b, recv_b, send_c, recv_c = sems
        others = (a + 1 - 2 * (a % 2), 3 - a, (a + 2) % 4)
        own, far = index(a, b), index(a, 1 - b)

        def bias_copy(place, send, device):
            spot = 2 * place + core
            return remote(full.at[spot], full.at[spot], send_b.at[send], recv_b.at[place], device)

        def copy_to_sibling(place):
            spot = 2 * place + core
            return remote(full.at[spot], full.at[spot], send_c.at[place], recv_c.at[place], sibling)

        def from_sibling(place):
            spot = 2 * place + 1 - core
            return remote(full.at[spot], full.at[spot], send_c.at[place], recv_c.at[place], sibling)

        def pass_on(place):
            bias_copy(place, 0, mate).wait_recv()
            copy_to_sibling(place).start()

        shift_bias(line, full, 2 * own + core)
        bias_copy(own, 0, mate).start()
        for k, other in enumerate(others):
            bias_copy(own, 1 + k, device_of(other)).start()
        copy_to_sibling(own).start()
        pass_on(far)
        for k, other in enumerate(others):
            bias_copy(far, 4 + k, device_of(other)).start()
        ready()

        def one_row(i, carry):
            prepare(i, whole[i], project[...], gate_bias[...], query, key, value, gate)
            return carry

        lax.fori_loop(0, 4, one_row, 0)
        for other in others:
            pass_on(index(other, b))

        def chunk(t, carry):
            half = (a // 2 + t + lane) % 2
            side = (b + t // 2) % 2
            pair = (index(2 * half, side), index(2 * half + 1, side))
            for place in pair:
                from_sibling(place).wait_recv()
            for i in range(4):
                attend(i, pair, full, query, key, value, gate, gated)
            for place in pair:
                send_home(place)

            @pl.when(t == 1)
            def _():
                for other in others:
                    pass_on(index(other, 1 - b))

            return carry

        lax.fori_loop(0, 4, chunk, 0)
        bias_copy(own, 0, mate).wait_send()
        for k, other in enumerate(others):
            bias_copy(own, 1 + k, device_of(other)).wait_send()
            bias_copy(far, 4 + k, device_of(other)).wait_send()
        for place in range(8):
            copy_to_sibling(place).wait_send()

    weight = spread_weight(bias_s[...])

    def norm_start(t, carry):
        normed = layer_norm(pair[pl.ds(pl.multiple_of(t * 256, 256), 256)], gain_s[...])
        normed_s[pl.ds(t * 8, 8)] = normed.reshape(8, 32, 128)
        mine_s[pl.ds(pl.multiple_of(t * 8, 8), 8)] = bias_rows(normed, weight, 8)
        return carry

    lax.fori_loop(0, 8, norm_start, 0)

    pl.semaphore_wait(barrier, 23)

    def line_copy_s(s):
        p = (c + s) % 16
        return remote(
            mine_s.at[pl.ds(pl.multiple_of(32 * (p % 2), 32), 32)], line_s.at[c],
            send_l_s.at[s], recv_l_s.at[s], {"col": p},
        )

    def tile_copy_s(s):
        p = (c + s) % 16
        return remote(
            normed_s.at[pl.ds(4 * p, 4)], whole_s.at[:, pl.ds(pl.multiple_of(32 * c, 32), 32)],
            send_x_s.at[s], recv_x_s.at[s], {"col": p},
        )

    for s in range(1, 16):
        line_copy_s(s).start()
    for s in range(1, 16):
        tile_copy_s(s).start()
    line_s[c] = mine_s[pl.ds(pl.multiple_of(32 * core, 32), 32)]
    whole_s[:, pl.ds(pl.multiple_of(32 * c, 32), 32)] = normed_s[pl.ds(4 * c, 4)]
    for s in range(1, 16):
        line_copy_s(s).wait_recv()

    def ready_s():
        for s in range(1, 16):
            tile_copy_s(s).wait_recv()

    def home_copy_s(p):
        return remote(
            gated_s.at[:, pl.ds(pl.multiple_of(32 * p, 32), 32)], home_s.at[pl.ds(4 * c, 4)],
            send_h_s.at[p], recv_h_s.at[c], {"col": p},
        )

    def send_home_s(place):
        for u in range(2):
            p = 2 * place + u

            @pl.when(p != c)
            def _():
                home_copy_s(p).start()

            @pl.when(p == c)
            def _():
                home_s[pl.ds(4 * c, 4)] = gated_s[:, pl.ds(pl.multiple_of(32 * c, 32), 32)]

    ring_s = (x, y_lo, z, lambda a, b: 4 * b + a, lambda a: {"row": 4 * y_lo + a}, above)
    attention(
        ring_s, line_s, whole_s, project_s, gate_bias_s, full_s, gated_s,
        (send_b_s, recv_b_s, send_c_s, recv_c_s), ready_s, send_home_s,
    )

    weight_e = spread_weight(bias_e[...])
    late_s = ((c // 4) % 2 + x // 2) % 2
    lane = lax.broadcasted_iota(jnp.int32, (32, 128), 1) % 32

    def residual(e, carry):
        part = (late_s + e // 2) % 2 + 2 * (e % 2)
        for u in range(4):
            p = 4 * part + u

            @pl.when(p != c)
            def _():
                remote(
                    gated_s.at[:, pl.ds(0, 32)], home_s.at[pl.ds(4 * p, 4)],
                    send_h_s.at[p], recv_h_s.at[p], {"col": p},
                ).wait_recv()

        rows = pl.ds(pl.multiple_of(part * 512, 512), 512)
        update = jnp.dot(
            home_s[pl.ds(part * 16, 16)].reshape(512, 128), out_s[...], preferred_element_type=F32
        )
        total = pair[rows] + update
        first[rows] = total
        normed = layer_norm(total, gain_e[...])
        swap[rows] = normed.astype(F32)
        every = bias_all(normed, weight_e).reshape(16, 32, 128)
        here = lane - 16 * (part % 2)
        mixed = mine_e[part // 2]
        for u in range(16):
            mixed = jnp.where(here == u, every[u], mixed)
        mine_e[part // 2] = mixed
        return carry

    lax.fori_loop(0, 4, residual, 0)

    def line_copy_e(s):
        p = (r + s) % 8
        return remote(mine_e, line_e.at[pl.ds(2 * r, 2)], send_l_e.at[s], recv_l_e.at[s], {"row": p})

    def tile_copy_e(s):
        p = (r + s) % 8
        return remote(
            normed_e.at[pl.ds(4 * p, 4)], whole_e.at[:, pl.ds(pl.multiple_of(64 * r, 64), 64)],
            send_x_e.at[s], recv_x_e.at[s], {"row": p},
        )

    for s in range(1, 8):
        line_copy_e(s).start()

    def turned(t, carry):
        for u in range(8):
            normed_e[t * 8 + u] = swap[pl.ds(t * 8 + u, 64, stride=32)].astype(BF16)
        return carry

    lax.fori_loop(0, 4, turned, 0)
    for s in range(1, 8):
        tile_copy_e(s).start()
    line_e[pl.ds(2 * r, 2)] = mine_e[...]
    whole_e[:, pl.ds(pl.multiple_of(64 * r, 64), 64)] = normed_e[pl.ds(4 * r, 4)]
    for s in range(1, 8):
        line_copy_e(s).wait_recv()

    def ready_e():
        for s in range(1, 8):
            tile_copy_e(s).wait_recv()

    def home_copy_e(p):
        return remote(
            gated_e.at[:, pl.ds(pl.multiple_of(64 * p, 64), 64)], home_e.at[pl.ds(4 * r, 4)],
            send_h_e.at[p], recv_h_e.at[r], {"row": p},
        )

    def send_home_e(p):
        @pl.when(p != r)
        def _():
            home_copy_e(p).start()

        @pl.when(p == r)
        def _():
            home_e[pl.ds(4 * r, 4)] = gated_e[:, pl.ds(pl.multiple_of(64 * r, 64), 64)]

    ring_e = (z, y_hi, r // 2, lambda a, b: 2 * a + b, lambda a: {"col": 4 * a + 2 * y_hi + core}, across)
    attention(
        ring_e, line_e, whole_e, project_e, gate_bias_e, full_e, gated_e,
        (send_b_e, recv_b_e, send_c_e, recv_c_e), ready_e, send_home_e,
    )

    late_e = (y_lo + z // 2) % 2

    def finish(e, carry):
        part = (late_e + e // 2) % 2 + 2 * (e % 2)
        for u in range(2):
            p = 2 * part + u

            @pl.when(p != r)
            def _():
                remote(
                    gated_e.at[:, pl.ds(0, 64)], home_e.at[pl.ds(4 * p, 4)],
                    send_h_e.at[p], recv_h_e.at[p], {"row": p},
                ).wait_recv()

        update = jnp.dot(
            home_e[pl.ds(part * 8, 8)].reshape(512, 128), out_e[...], preferred_element_type=F32
        )
        for u in range(8):
            rows = pl.ds(part * 8 + u, 64, stride=32)
            result[rows] = first[rows] + update[64 * u : 64 * (u + 1)]
        return carry

    lax.fori_loop(0, 4, finish, 0)

    for s in range(1, 16):
        line_copy_s(s).wait_send()
        tile_copy_s(s).wait_send()
        home_copy_s((c + s) % 16).wait_send()
    for s in range(1, 8):
        line_copy_e(s).wait_send()
        tile_copy_e(s).wait_send()
        home_copy_e((r + s) % 8).wait_send()


def local(pair, gain_s, project_s, gate_bias_s, bias_s, out_s, gain_e, project_e, gate_bias_e, bias_e, out_e):
    vmem = pl.BlockSpec(memory_space=pltpu.VMEM)
    dma = pltpu.SemaphoreType.DMA
    out = pl.pallas_call(
        kernel,
        out_shape=jax.ShapeDtypeStruct((2048, 128), F32),
        in_specs=[vmem] * 11,
        out_specs=vmem,
        scratch_shapes=[
            pltpu.VMEM((64, 32, 128), BF16),
            pltpu.VMEM((32, 64, 128), BF16),
            pltpu.VMEM((64, 128), F32),
            pltpu.VMEM((2, 32, 128), F32),
            pltpu.VMEM((16, 32, 128), F32),
            pltpu.VMEM((16, 32, 128), F32),
            pltpu.VMEM((4, 512, 128), BF16),
            pltpu.VMEM((4, 512, 128), BF16),
            pltpu.VMEM((16, 16, 32, 128), BF16),
            pltpu.VMEM((16, 16, 32, 128), BF16),
            pltpu.VMEM((4, 512, 128), BF16),
            pltpu.VMEM((4, 16, 4, 32, 128), BF16),
            pltpu.VMEM((4, 16, 4, 32, 256), BF16),
            pltpu.VMEM((4, 512, 128), F32),
            pltpu.VMEM((4, 512, 128), BF16),
            pltpu.VMEM((4, 512, 128), BF16),
            pltpu.VMEM((64, 32, 128), BF16),
            pltpu.VMEM((32, 64, 128), BF16),
            pltpu.VMEM((2048, 128), F32),
            pltpu.VMEM((2048, 128), F32),
        ]
        + [dma((n,)) for n in (16, 16, 8, 8) * 2 + (8,) * 8 + (16, 16, 8, 8)],
        compiler_params=pltpu.CompilerParams(
            collective_id=0, has_side_effects=True, vmem_limit_bytes=56 * 2**20
        ),
    )(
        pair.reshape(2048, 128),
        gain_s.reshape(1, 128), project_s, gate_bias_s.reshape(1, 128), bias_s.T, out_s,
        gain_e.reshape(1, 128), project_e, gate_bias_e.reshape(1, 128), bias_e.T, out_e,
    )
    return out.reshape(pair.shape)


def solution(mesh):
    return jax.shard_map(
        local,
        mesh=mesh,
        in_specs=(P("row", "col", None), P(), P(), P(), P(), P(), P(), P(), P(), P(), P()),
        out_specs=P("row", "col", None),
        check_vma=False,
    )
```

```python
import functools

import jax
import jax.numpy as jnp
from jax import lax
from jax.experimental import pallas as pl
from jax.experimental.pallas import tpu as pltpu
from jax.sharding import PartitionSpec as P

MESH = pl.DeviceIdType.MESH
LOG2E = 1.4426950408889634
BF16 = jnp.bfloat16
F32 = jnp.float32


def layer_norm(values, gain):
    centred = values - jnp.mean(values, axis=-1, keepdims=True)
    variance = jnp.mean(centred * centred, axis=-1, keepdims=True)
    return (centred * lax.rsqrt(variance + 1e-05) * gain).astype(BF16)


def head_max(values):
    turned = values.T
    rows = turned.shape[1]
    turned = jnp.max(turned.reshape(4, 32, rows), axis=1, keepdims=True)
    return jnp.broadcast_to(turned, (4, 32, rows)).reshape(128, rows).T


def spread_weight(weight):
    head = lax.broadcasted_iota(jnp.int32, (128, 128), 0) // 32
    weight = weight.astype(F32)
    out = jnp.zeros((128, 128), F32)
    for h in range(4):
        out = jnp.where(head == h, weight[h : h + 1], out)
    return out.astype(BF16)


def bias_all(normed, weight):
    dims = (((1,), (1,)), ((), ()))
    return lax.dot_general(normed, weight, dims, preferred_element_type=F32) * LOG2E


def bias_rows(normed, weight, rows):
    every = bias_all(normed, weight)
    k_lane = lax.broadcasted_iota(jnp.int32, (1, 32, 128), 2) % 32
    k_row = lax.broadcasted_iota(jnp.int32, (1, 32, 128), 1)
    return jnp.sum(jnp.where(k_lane == k_row, every.reshape(rows, 32, 128), 0.0), axis=1)


def prepare(index, x, project, gate_bias, query, key, value, gate):
    projected = jnp.dot(x, project, preferred_element_type=F32)
    query[index] = (projected[:, :128] * (32**-0.5 * LOG2E)).astype(BF16)
    gate[index] = jax.nn.sigmoid(projected[:, 384:] + gate_bias)
    keys = projected[:, 128:256].astype(BF16).reshape(16, 32, 128)
    values = projected[:, 256:384].astype(BF16).reshape(16, 32, 128)
    head = lax.broadcasted_iota(jnp.int32, (1, 32, 128), 2) // 32
    for h in range(4):
        key[index, :, h] = jnp.where(head == h, keys, jnp.zeros_like(keys))
        value[index, :, h, :, :128] = jnp.where(head == h, values, jnp.zeros_like(values))


def attend(index, pair, bias, query, key, value, gate, out):
    rows = [pl.ds(pl.multiple_of(64 * place, 64), 64) for place in pair]
    scores = lax.dot_general(
        jnp.concatenate([query[index, at] for at in rows], axis=0),
        key[index].reshape(2048, 128),
        (((1,), (1,)), ((), ())),
        preferred_element_type=F32,
    )
    parts = []
    for b in range(16):
        added = [bias[pl.ds(2 * place, 2), b].reshape(64, 128) for place in pair]
        parts.append(scores[:, 128 * b : 128 * (b + 1)] + jnp.concatenate(added, axis=0).astype(F32))
    high = head_max(functools.reduce(jnp.maximum, parts))
    expo = jnp.concatenate([jnp.exp2(part - high).astype(BF16) for part in parts], axis=1)
    both = jnp.dot(expo, value[index].reshape(2048, 256), preferred_element_type=F32)
    mean = both[:, :128] / both[:, 128:]
    for u, at in enumerate(rows):
        out[index, at] = (gate[index, at] * mean[64 * u : 64 * (u + 1)]).astype(BF16)


def shift_bias(line, full, slot):
    values = line[...]
    full[slot] = (values - head_max(jnp.max(values, axis=0))[None]).astype(BF16)


def remote(src, dst, send, recv, device):
    return pltpu.make_async_remote_copy(
        src_ref=src, dst_ref=dst, send_sem=send, recv_sem=recv, device_id=device, device_id_type=MESH
    )


def kernel(
    pair, gain_s, project_s, gate_bias_s, bias_s, out_s, gain_e, project_e, gate_bias_e, bias_e, out_e,
    result,
    normed_s, normed_e, mine_s, mine_e, line_s, line_e, whole_s, whole_e, full_s, full_e,
    query, key, value, gate, gated_s, gated_e, home_s, home_e, first, swap,
    send_x_s, recv_x_s, send_x_e, recv_x_e, send_l_s, recv_l_s, send_l_e, recv_l_e,
    send_b_s, recv_b_s, send_b_e, recv_b_e, send_c_s, recv_c_s, send_c_e, recv_c_e,
    send_h_s, recv_h_s, send_h_e, recv_h_e,
):
    r = lax.axis_index("row")
    c = lax.axis_index("col")
    core = c % 2
    sibling = {"col": c + 1 - 2 * core}
    x, y_lo = r % 4, r // 4
    z, y_hi = c // 4, (c // 2) % 2

    across = {"row": 4 * (1 - y_lo) + x, "col": 4 * z + 2 * (1 - y_hi) + core}
    above = {"row": 4 * (1 - y_lo) + x, "col": 4 * z + 2 * ((y_hi + y_lo) % 2) + core}

    barrier = pltpu.get_barrier_semaphore()
    for s in range(1, 16):
        pl.semaphore_signal(barrier, inc=1, device_id={"col": (c + s) % 16}, device_id_type=MESH)
    for s in range(1, 8):
        pl.semaphore_signal(barrier, inc=1, device_id={"row": (r + s) % 8}, device_id_type=MESH)
    pl.semaphore_signal(barrier, inc=1, device_id=across, device_id_type=MESH)

    mine_e[...] = jnp.zeros_like(mine_e)
    head = lax.broadcasted_iota(jnp.int32, (1, 32, 128), 2) // 32
    for i in range(4):
        for h in range(4):
            value[i, :, h, :, 128:] = jnp.broadcast_to(
                jnp.where(head == h, 1.0, 0.0).astype(BF16), (16, 32, 128)
            )


    def attention(ring, line, whole, project, gate_bias, full, gated, sems, ready, send_home):
        a, b, last, index, device_of, mate = ring
        send_b, recv_b, send_c, recv_c = sems
        others = ((a + 2) % 4, a + 1 - 2 * (a % 2), 3 - a)
        own, far = index(a, b), index(a, 1 - b)

        def bias_copy(place, send, device):
            spot = 2 * place + core
            return remote(full.at[spot], full.at[spot], send_b.at[send], recv_b.at[place], device)

        def copy_to_sibling(place):
            spot = 2 * place + core
            return remote(full.at[spot], full.at[spot], send_c.at[place], recv_c.at[place], sibling)

        def from_sibling(place):
            spot = 2 * place + 1 - core
            return remote(full.at[spot], full.at[spot], send_c.at[place], recv_c.at[place], sibling)

        def pass_on(place):
            bias_copy(place, 0, mate).wait_recv()
            copy_to_sibling(place).start()

        shift_bias(line, full, 2 * own + core)
        bias_copy(own, 0, mate).start()
        for k, other in enumerate(others):
            bias_copy(own, 1 + k, device_of(other)).start()
        copy_to_sibling(own).start()
        pass_on(far)
        for k, other in enumerate(others):
            bias_copy(far, 4 + k, device_of(other)).start()
        ready()

        def one_row(i, carry):
            prepare(i, whole[i], project[...], gate_bias[...], query, key, value, gate)
            return carry

        lax.fori_loop(0, 4, one_row, 0)
        for other in others:
            pass_on(index(other, b))

        def chunk(t, carry):
            half = (last + t + 1) % 2
            side = (b + t // 2) % 2
            pair = (index(2 * half, side), index(2 * half + 1, side))
            for place in pair:
                from_sibling(place).wait_recv()
            for i in range(4):
                attend(i, pair, full, query, key, value, gate, gated)
            for place in pair:
                send_home(place)

            @pl.when(t == 1)
            def _():
                for other in others:
                    pass_on(index(other, 1 - b))

            return carry

        lax.fori_loop(0, 4, chunk, 0)
        bias_copy(own, 0, mate).wait_send()
        for k, other in enumerate(others):
            bias_copy(own, 1 + k, device_of(other)).wait_send()
            bias_copy(far, 4 + k, device_of(other)).wait_send()
        for place in range(8):
            copy_to_sibling(place).wait_send()

    weight = spread_weight(bias_s[...])

    def norm_start(t, carry):
        normed = layer_norm(pair[pl.ds(pl.multiple_of(t * 256, 256), 256)], gain_s[...])
        normed_s[pl.ds(t * 8, 8)] = normed.reshape(8, 32, 128)
        mine_s[pl.ds(pl.multiple_of(t * 8, 8), 8)] = bias_rows(normed, weight, 8)
        return carry

    lax.fori_loop(0, 8, norm_start, 0)

    pl.semaphore_wait(barrier, 23)

    def line_copy_s(s):
        p = (c + s) % 16
        return remote(
            mine_s.at[pl.ds(pl.multiple_of(32 * (p % 2), 32), 32)], line_s.at[c],
            send_l_s.at[s], recv_l_s.at[s], {"col": p},
        )

    def tile_copy_s(s):
        p = (c + s) % 16
        return remote(
            normed_s.at[pl.ds(4 * p, 4)], whole_s.at[:, pl.ds(pl.multiple_of(32 * c, 32), 32)],
            send_x_s.at[s], recv_x_s.at[s], {"col": p},
        )

    for s in range(1, 16):
        line_copy_s(s).start()
    for s in range(1, 16):
        tile_copy_s(s).start()
    line_s[c] = mine_s[pl.ds(pl.multiple_of(32 * core, 32), 32)]
    whole_s[:, pl.ds(pl.multiple_of(32 * c, 32), 32)] = normed_s[pl.ds(4 * c, 4)]
    for s in range(1, 16):
        line_copy_s(s).wait_recv()

    def ready_s():
        for s in range(1, 16):
            tile_copy_s(s).wait_recv()

    def home_copy_s(p):
        return remote(
            gated_s.at[:, pl.ds(pl.multiple_of(32 * p, 32), 32)], home_s.at[pl.ds(4 * c, 4)],
            send_h_s.at[p], recv_h_s.at[c], {"col": p},
        )

    def send_home_s(place):
        for u in range(2):
            p = 2 * place + u

            @pl.when(p != c)
            def _():
                home_copy_s(p).start()

            @pl.when(p == c)
            def _():
                home_s[pl.ds(4 * c, 4)] = gated_s[:, pl.ds(pl.multiple_of(32 * c, 32), 32)]

    ring_s = (x, y_lo, (z + z // 2 + 1 - y_lo) % 2, lambda a, b: 4 * b + a, lambda a: {"row": 4 * y_lo + a}, above)
    attention(
        ring_s, line_s, whole_s, project_s, gate_bias_s, full_s, gated_s,
        (send_b_s, recv_b_s, send_c_s, recv_c_s), ready_s, send_home_s,
    )

    weight_e = spread_weight(bias_e[...])
    lane = lax.broadcasted_iota(jnp.int32, (32, 128), 1) % 32

    def residual(e, carry):
        plane = z + (1 - e // 2) * (1 - 2 * (z % 2))
        part = plane + (e % 2) * (3 - 2 * plane)
        for u in range(4):
            p = 4 * part + u

            @pl.when(p != c)
            def _():
                remote(
                    gated_s.at[:, pl.ds(0, 32)], home_s.at[pl.ds(4 * p, 4)],
                    send_h_s.at[p], recv_h_s.at[p], {"col": p},
                ).wait_recv()

        rows = pl.ds(pl.multiple_of(part * 512, 512), 512)
        update = jnp.dot(
            home_s[pl.ds(part * 16, 16)].reshape(512, 128), out_s[...], preferred_element_type=F32
        )
        total = pair[rows] + update
        first[rows] = total
        normed = layer_norm(total, gain_e[...])
        swap[rows] = normed.astype(F32)
        every = bias_all(normed, weight_e).reshape(16, 32, 128)
        here = lane - 16 * (part % 2)
        mixed = mine_e[part // 2]
        for u in range(16):
            mixed = jnp.where(here == u, every[u], mixed)
        mine_e[part // 2] = mixed
        return carry

    lax.fori_loop(0, 4, residual, 0)

    def line_copy_e(s):
        p = (r + s) % 8
        return remote(mine_e, line_e.at[pl.ds(2 * r, 2)], send_l_e.at[s], recv_l_e.at[s], {"row": p})

    def tile_copy_e(s):
        p = (r + s) % 8
        return remote(
            normed_e.at[pl.ds(4 * p, 4)], whole_e.at[:, pl.ds(pl.multiple_of(64 * r, 64), 64)],
            send_x_e.at[s], recv_x_e.at[s], {"row": p},
        )

    for s in range(1, 8):
        line_copy_e(s).start()

    def turned(t, carry):
        for u in range(8):
            normed_e[t * 8 + u] = swap[pl.ds(t * 8 + u, 64, stride=32)].astype(BF16)
        return carry

    lax.fori_loop(0, 4, turned, 0)
    for s in range(1, 8):
        tile_copy_e(s).start()
    line_e[pl.ds(2 * r, 2)] = mine_e[...]
    whole_e[:, pl.ds(pl.multiple_of(64 * r, 64), 64)] = normed_e[pl.ds(4 * r, 4)]
    for s in range(1, 8):
        line_copy_e(s).wait_recv()

    def ready_e():
        for s in range(1, 8):
            tile_copy_e(s).wait_recv()

    def home_copy_e(p):
        return remote(
            gated_e.at[:, pl.ds(pl.multiple_of(64 * p, 64), 64)], home_e.at[pl.ds(4 * r, 4)],
            send_h_e.at[p], recv_h_e.at[r], {"row": p},
        )

    def send_home_e(p):
        @pl.when(p != r)
        def _():
            home_copy_e(p).start()

        @pl.when(p == r)
        def _():
            home_e[pl.ds(4 * r, 4)] = gated_e[:, pl.ds(pl.multiple_of(64 * r, 64), 64)]

    ring_e = (z, y_hi, y_lo, lambda a, b: 2 * a + b, lambda a: {"col": 4 * a + 2 * y_hi + core}, across)
    attention(
        ring_e, line_e, whole_e, project_e, gate_bias_e, full_e, gated_e,
        (send_b_e, recv_b_e, send_c_e, recv_c_e), ready_e, send_home_e,
    )

    def finish(e, carry):
        part = 2 * ((y_lo + 1 + e // 2) % 2) + e % 2
        for u in range(2):
            p = 2 * part + u

            @pl.when(p != r)
            def _():
                remote(
                    gated_e.at[:, pl.ds(0, 64)], home_e.at[pl.ds(4 * p, 4)],
                    send_h_e.at[p], recv_h_e.at[p], {"row": p},
                ).wait_recv()

        update = jnp.dot(
            home_e[pl.ds(part * 8, 8)].reshape(512, 128), out_e[...], preferred_element_type=F32
        )
        for u in range(8):
            rows = pl.ds(part * 8 + u, 64, stride=32)
            result[rows] = first[rows] + update[64 * u : 64 * (u + 1)]
        return carry

    lax.fori_loop(0, 4, finish, 0)

    for s in range(1, 16):
        line_copy_s(s).wait_send()
        tile_copy_s(s).wait_send()
        home_copy_s((c + s) % 16).wait_send()
    for s in range(1, 8):
        line_copy_e(s).wait_send()
        tile_copy_e(s).wait_send()
        home_copy_e((r + s) % 8).wait_send()


def local(pair, gain_s, project_s, gate_bias_s, bias_s, out_s, gain_e, project_e, gate_bias_e, bias_e, out_e):
    vmem = pl.BlockSpec(memory_space=pltpu.VMEM)
    dma = pltpu.SemaphoreType.DMA
    out = pl.pallas_call(
        kernel,
        out_shape=jax.ShapeDtypeStruct((2048, 128), F32),
        in_specs=[vmem] * 11,
        out_specs=vmem,
        scratch_shapes=[
            pltpu.VMEM((64, 32, 128), BF16),
            pltpu.VMEM((32, 64, 128), BF16),
            pltpu.VMEM((64, 128), F32),
            pltpu.VMEM((2, 32, 128), F32),
            pltpu.VMEM((16, 32, 128), F32),
            pltpu.VMEM((16, 32, 128), F32),
            pltpu.VMEM((4, 512, 128), BF16),
            pltpu.VMEM((4, 512, 128), BF16),
            pltpu.VMEM((16, 16, 32, 128), BF16),
            pltpu.VMEM((16, 16, 32, 128), BF16),
            pltpu.VMEM((4, 512, 128), BF16),
            pltpu.VMEM((4, 16, 4, 32, 128), BF16),
            pltpu.VMEM((4, 16, 4, 32, 256), BF16),
            pltpu.VMEM((4, 512, 128), F32),
            pltpu.VMEM((4, 512, 128), BF16),
            pltpu.VMEM((4, 512, 128), BF16),
            pltpu.VMEM((64, 32, 128), BF16),
            pltpu.VMEM((32, 64, 128), BF16),
            pltpu.VMEM((2048, 128), F32),
            pltpu.VMEM((2048, 128), F32),
        ]
        + [dma((n,)) for n in (16, 16, 8, 8) * 2 + (8,) * 8 + (16, 16, 8, 8)],
        compiler_params=pltpu.CompilerParams(
            collective_id=0, has_side_effects=True, vmem_limit_bytes=56 * 2**20
        ),
    )(
        pair.reshape(2048, 128),
        gain_s.reshape(1, 128), project_s, gate_bias_s.reshape(1, 128), bias_s.T, out_s,
        gain_e.reshape(1, 128), project_e, gate_bias_e.reshape(1, 128), bias_e.T, out_e,
    )
    return out.reshape(pair.shape)


def solution(mesh):
    return jax.shard_map(
        local,
        mesh=mesh,
        in_specs=(P("row", "col", None), P(), P(), P(), P(), P(), P(), P(), P(), P(), P()),
        out_specs=P("row", "col", None),
        check_vma=False,
    )
```

```python
import functools

import jax
import jax.numpy as jnp
from jax import lax
from jax.experimental import pallas as pl
from jax.experimental.pallas import tpu as pltpu
from jax.sharding import PartitionSpec as P

MESH = pl.DeviceIdType.MESH
LOG2E = 1.4426950408889634
BF16 = jnp.bfloat16
F32 = jnp.float32


def layer_norm(values, gain):
    centred = values - jnp.mean(values, axis=-1, keepdims=True)
    variance = jnp.mean(centred * centred, axis=-1, keepdims=True)
    return (centred * lax.rsqrt(variance + 1e-05) * gain).astype(BF16)


def head_max(values):
    turned = values.T
    rows = turned.shape[1]
    turned = jnp.max(turned.reshape(4, 32, rows), axis=1, keepdims=True)
    return jnp.broadcast_to(turned, (4, 32, rows)).reshape(128, rows).T


def spread_weight(weight):
    head = lax.broadcasted_iota(jnp.int32, (128, 128), 0) // 32
    weight = weight.astype(F32)
    out = jnp.zeros((128, 128), F32)
    for h in range(4):
        out = jnp.where(head == h, weight[h : h + 1], out)
    return out.astype(BF16)


def bias_all(normed, weight):
    dims = (((1,), (1,)), ((), ()))
    return lax.dot_general(normed, weight, dims, preferred_element_type=F32) * LOG2E


def bias_rows(normed, weight, rows):
    every = bias_all(normed, weight)
    k_lane = lax.broadcasted_iota(jnp.int32, (1, 32, 128), 2) % 32
    k_row = lax.broadcasted_iota(jnp.int32, (1, 32, 128), 1)
    return jnp.sum(jnp.where(k_lane == k_row, every.reshape(rows, 32, 128), 0.0), axis=1)


def prepare(index, x, project, gate_bias, query, key, value, gate):
    projected = jnp.dot(x, project, preferred_element_type=F32)
    query[index] = (projected[:, :128] * (32**-0.5 * LOG2E)).astype(BF16)
    gate[index] = jax.nn.sigmoid(projected[:, 384:] + gate_bias)
    keys = projected[:, 128:256].astype(BF16).reshape(16, 32, 128)
    values = projected[:, 256:384].astype(BF16).reshape(16, 32, 128)
    head = lax.broadcasted_iota(jnp.int32, (1, 32, 128), 2) // 32
    for h in range(4):
        key[index, :, h] = jnp.where(head == h, keys, jnp.zeros_like(keys))
        value[index, :, h, :, :128] = jnp.where(head == h, values, jnp.zeros_like(values))


def attend(index, pair, bias, query, key, value, gate, out):
    rows = [pl.ds(pl.multiple_of(64 * place, 64), 64) for place in pair]
    scores = lax.dot_general(
        jnp.concatenate([query[index, at] for at in rows], axis=0),
        key[index].reshape(2048, 128),
        (((1,), (1,)), ((), ())),
        preferred_element_type=F32,
    )
    parts = []
    for b in range(16):
        added = [bias[pl.ds(2 * place, 2), b].reshape(64, 128) for place in pair]
        parts.append(scores[:, 128 * b : 128 * (b + 1)] + jnp.concatenate(added, axis=0).astype(F32))
    high = head_max(functools.reduce(jnp.maximum, parts))
    expo = jnp.concatenate([jnp.exp2(part - high).astype(BF16) for part in parts], axis=1)
    both = jnp.dot(expo, value[index].reshape(2048, 256), preferred_element_type=F32)
    mean = both[:, :128] / both[:, 128:]
    for u, at in enumerate(rows):
        out[index, at] = (gate[index, at] * mean[64 * u : 64 * (u + 1)]).astype(BF16)


def shift_bias(line, full, slot):
    values = line[...]
    full[slot] = (values - head_max(jnp.max(values, axis=0))[None]).astype(BF16)


def remote(src, dst, send, recv, device):
    return pltpu.make_async_remote_copy(
        src_ref=src, dst_ref=dst, send_sem=send, recv_sem=recv, device_id=device, device_id_type=MESH
    )


def kernel(
    pair, gain_s, project_s, gate_bias_s, bias_s, out_s, gain_e, project_e, gate_bias_e, bias_e, out_e,
    result,
    normed_s, normed_e, mine_s, mine_e, line_s, line_e, whole_s, whole_e, full_s, full_e,
    query, key, value, gate, gated_s, gated_e, home_s, home_e, first, swap,
    send_x_s, recv_x_s, send_x_e, recv_x_e, send_l_s, recv_l_s, send_l_e, recv_l_e,
    send_b_s, recv_b_s, send_b_e, recv_b_e, send_c_s, recv_c_s, send_c_e, recv_c_e,
    send_h_s, recv_h_s, send_h_e, recv_h_e,
):
    r = lax.axis_index("row")
    c = lax.axis_index("col")
    core = c % 2
    sibling = {"col": c + 1 - 2 * core}
    x, y_lo = r % 4, r // 4
    z, y_hi = c // 4, (c // 2) % 2

    across = {"row": 4 * (1 - y_lo) + x, "col": 4 * z + 2 * (1 - y_hi) + core}
    above = {"row": 4 * (1 - y_lo) + x, "col": 4 * z + 2 * ((y_hi + y_lo) % 2) + core}

    barrier = pltpu.get_barrier_semaphore()
    for s in (10, 11, 9, 6, 7, 5, 14, 15, 13, 8, 2, 3, 4, 12, 1):
        pl.semaphore_signal(barrier, inc=1, device_id={"col": (c + s) % 16}, device_id_type=MESH)
    for s in range(1, 8):
        pl.semaphore_signal(barrier, inc=1, device_id={"row": (r + s) % 8}, device_id_type=MESH)
    pl.semaphore_signal(barrier, inc=1, device_id=across, device_id_type=MESH)

    mine_e[...] = jnp.zeros_like(mine_e)
    head = lax.broadcasted_iota(jnp.int32, (1, 32, 128), 2) // 32
    for i in range(4):
        for h in range(4):
            value[i, :, h, :, 128:] = jnp.broadcast_to(
                jnp.where(head == h, 1.0, 0.0).astype(BF16), (16, 32, 128)
            )


    def attention(ring, line, whole, project, gate_bias, full, gated, sems, ready, send_home):
        a, b, last, index, device_of, mate = ring
        send_b, recv_b, send_c, recv_c = sems
        others = ((a + 2) % 4, a + 1 - 2 * (a % 2), 3 - a)
        own, far = index(a, b), index(a, 1 - b)

        def bias_copy(place, send, device):
            spot = 2 * place + core
            return remote(full.at[spot], full.at[spot], send_b.at[send], recv_b.at[place], device)

        def copy_to_sibling(place):
            spot = 2 * place + core
            return remote(full.at[spot], full.at[spot], send_c.at[place], recv_c.at[place], sibling)

        def from_sibling(place):
            spot = 2 * place + 1 - core
            return remote(full.at[spot], full.at[spot], send_c.at[place], recv_c.at[place], sibling)

        def pass_on(place):
            bias_copy(place, 0, mate).wait_recv()
            copy_to_sibling(place).start()

        shift_bias(line, full, 2 * own + core)
        bias_copy(own, 0, mate).start()
        for k, other in enumerate(others):
            bias_copy(own, 1 + k, device_of(other)).start()
        copy_to_sibling(own).start()
        pass_on(far)
        for k, other in enumerate(others):
            bias_copy(far, 4 + k, device_of(other)).start()
        ready()

        def one_row(i, carry):
            prepare(i, whole[i], project[...], gate_bias[...], query, key, value, gate)
            return carry

        lax.fori_loop(0, 4, one_row, 0)
        for other in others:
            pass_on(index(other, b))

        def chunk(places):
            for place in places:
                from_sibling(place).wait_recv()
            for i in range(4):
                attend(i, places, full, query, key, value, gate, gated)
            for place in places:
                send_home(place)

        chunk([index(k, b) for k in range(4)])
        for other in others:
            pass_on(index(other, 1 - b))

        def far_chunk(t, carry):
            half = (last + 1 + t) % 2
            chunk([index(2 * half, 1 - b), index(2 * half + 1, 1 - b)])
            return carry

        lax.fori_loop(0, 2, far_chunk, 0)
        bias_copy(own, 0, mate).wait_send()
        for k, other in enumerate(others):
            bias_copy(own, 1 + k, device_of(other)).wait_send()
            bias_copy(far, 4 + k, device_of(other)).wait_send()
        for place in range(8):
            copy_to_sibling(place).wait_send()

    weight = spread_weight(bias_s[...])

    def norm_start(t, carry):
        normed = layer_norm(pair[pl.ds(pl.multiple_of(t * 256, 256), 256)], gain_s[...])
        normed_s[pl.ds(t * 8, 8)] = normed.reshape(8, 32, 128)
        mine_s[pl.ds(pl.multiple_of(t * 8, 8), 8)] = bias_rows(normed, weight, 8)
        return carry

    lax.fori_loop(0, 8, norm_start, 0)

    pl.semaphore_wait(barrier, 23)

    def line_copy_s(s):
        p = (c + s) % 16
        return remote(
            mine_s.at[pl.ds(pl.multiple_of(32 * (p % 2), 32), 32)], line_s.at[c],
            send_l_s.at[s], recv_l_s.at[s], {"col": p},
        )

    def tile_copy_s(s):
        p = (c + s) % 16
        return remote(
            normed_s.at[pl.ds(4 * p, 4)], whole_s.at[:, pl.ds(pl.multiple_of(32 * c, 32), 32)],
            send_x_s.at[s], recv_x_s.at[s], {"col": p},
        )

    for s in range(1, 16):
        line_copy_s(s).start()
    for s in range(1, 16):
        tile_copy_s(s).start()
    line_s[c] = mine_s[pl.ds(pl.multiple_of(32 * core, 32), 32)]
    whole_s[:, pl.ds(pl.multiple_of(32 * c, 32), 32)] = normed_s[pl.ds(4 * c, 4)]
    for s in range(1, 16):
        line_copy_s(s).wait_recv()

    def ready_s():
        for s in range(1, 16):
            tile_copy_s(s).wait_recv()

    def home_copy_s(p):
        return remote(
            gated_s.at[:, pl.ds(pl.multiple_of(32 * p, 32), 32)], home_s.at[pl.ds(4 * c, 4)],
            send_h_s.at[p], recv_h_s.at[c], {"col": p},
        )

    def send_home_s(place):
        for u in range(2):
            p = 2 * place + u

            @pl.when(p != c)
            def _():
                home_copy_s(p).start()

            @pl.when(p == c)
            def _():
                home_s[pl.ds(4 * c, 4)] = gated_s[:, pl.ds(pl.multiple_of(32 * c, 32), 32)]

    ring_s = (x, y_lo, (z + z // 2 + 1 - y_lo) % 2, lambda a, b: 4 * b + a, lambda a: {"row": 4 * y_lo + a}, above)
    attention(
        ring_s, line_s, whole_s, project_s, gate_bias_s, full_s, gated_s,
        (send_b_s, recv_b_s, send_c_s, recv_c_s), ready_s, send_home_s,
    )

    weight_e = spread_weight(bias_e[...])
    lane = lax.broadcasted_iota(jnp.int32, (32, 128), 1) % 32

    def residual(e, carry):
        plane = z + (1 - e // 2) * (1 - 2 * (z % 2))
        part = plane + (e % 2) * (3 - 2 * plane)
        for u in range(4):
            p = 4 * part + u

            @pl.when(p != c)
            def _():
                remote(
                    gated_s.at[:, pl.ds(0, 32)], home_s.at[pl.ds(4 * p, 4)],
                    send_h_s.at[p], recv_h_s.at[p], {"col": p},
                ).wait_recv()

        rows = pl.ds(pl.multiple_of(part * 512, 512), 512)
        update = jnp.dot(
            home_s[pl.ds(part * 16, 16)].reshape(512, 128), out_s[...], preferred_element_type=F32
        )
        total = pair[rows] + update
        first[rows] = total
        normed = layer_norm(total, gain_e[...])
        swap[rows] = normed.astype(F32)
        every = bias_all(normed, weight_e).reshape(16, 32, 128)
        here = lane - 16 * (part % 2)
        mixed = mine_e[part // 2]
        for u in range(16):
            mixed = jnp.where(here == u, every[u], mixed)
        mine_e[part // 2] = mixed
        return carry

    lax.fori_loop(0, 4, residual, 0)

    def line_copy_e(s):
        p = (r + s) % 8
        return remote(mine_e, line_e.at[pl.ds(2 * r, 2)], send_l_e.at[s], recv_l_e.at[s], {"row": p})

    def tile_copy_e(s):
        p = (r + s) % 8
        return remote(
            normed_e.at[pl.ds(4 * p, 4)], whole_e.at[:, pl.ds(pl.multiple_of(64 * r, 64), 64)],
            send_x_e.at[s], recv_x_e.at[s], {"row": p},
        )

    for s in range(1, 8):
        line_copy_e(s).start()

    def turned(t, carry):
        for u in range(8):
            normed_e[t * 8 + u] = swap[pl.ds(t * 8 + u, 64, stride=32)].astype(BF16)
        return carry

    lax.fori_loop(0, 4, turned, 0)
    for s in range(1, 8):
        tile_copy_e(s).start()
    line_e[pl.ds(2 * r, 2)] = mine_e[...]
    whole_e[:, pl.ds(pl.multiple_of(64 * r, 64), 64)] = normed_e[pl.ds(4 * r, 4)]
    for s in range(1, 8):
        line_copy_e(s).wait_recv()

    def ready_e():
        for s in range(1, 8):
            tile_copy_e(s).wait_recv()

    def home_copy_e(p):
        return remote(
            gated_e.at[:, pl.ds(pl.multiple_of(64 * p, 64), 64)], home_e.at[pl.ds(4 * r, 4)],
            send_h_e.at[p], recv_h_e.at[r], {"row": p},
        )

    def send_home_e(p):
        @pl.when(p != r)
        def _():
            home_copy_e(p).start()

        @pl.when(p == r)
        def _():
            home_e[pl.ds(4 * r, 4)] = gated_e[:, pl.ds(pl.multiple_of(64 * r, 64), 64)]

    ring_e = (z, y_hi, y_lo, lambda a, b: 2 * a + b, lambda a: {"col": 4 * a + 2 * y_hi + core}, across)
    attention(
        ring_e, line_e, whole_e, project_e, gate_bias_e, full_e, gated_e,
        (send_b_e, recv_b_e, send_c_e, recv_c_e), ready_e, send_home_e,
    )

    def finish(e, carry):
        part = 2 * ((y_lo + 1 + e // 2) % 2) + e % 2
        for u in range(2):
            p = 2 * part + u

            @pl.when(p != r)
            def _():
                remote(
                    gated_e.at[:, pl.ds(0, 64)], home_e.at[pl.ds(4 * p, 4)],
                    send_h_e.at[p], recv_h_e.at[p], {"row": p},
                ).wait_recv()

        update = jnp.dot(
            home_e[pl.ds(part * 8, 8)].reshape(512, 128), out_e[...], preferred_element_type=F32
        )
        for u in range(8):
            rows = pl.ds(part * 8 + u, 64, stride=32)
            result[rows] = first[rows] + update[64 * u : 64 * (u + 1)]
        return carry

    lax.fori_loop(0, 4, finish, 0)

    for s in range(1, 16):
        line_copy_s(s).wait_send()
        tile_copy_s(s).wait_send()
        home_copy_s((c + s) % 16).wait_send()
    for s in range(1, 8):
        line_copy_e(s).wait_send()
        tile_copy_e(s).wait_send()
        home_copy_e((r + s) % 8).wait_send()


def local(pair, gain_s, project_s, gate_bias_s, bias_s, out_s, gain_e, project_e, gate_bias_e, bias_e, out_e):
    vmem = pl.BlockSpec(memory_space=pltpu.VMEM)
    dma = pltpu.SemaphoreType.DMA
    out = pl.pallas_call(
        kernel,
        out_shape=jax.ShapeDtypeStruct((2048, 128), F32),
        in_specs=[vmem] * 11,
        out_specs=vmem,
        scratch_shapes=[
            pltpu.VMEM((64, 32, 128), BF16),
            pltpu.VMEM((32, 64, 128), BF16),
            pltpu.VMEM((64, 128), F32),
            pltpu.VMEM((2, 32, 128), F32),
            pltpu.VMEM((16, 32, 128), F32),
            pltpu.VMEM((16, 32, 128), F32),
            pltpu.VMEM((4, 512, 128), BF16),
            pltpu.VMEM((4, 512, 128), BF16),
            pltpu.VMEM((16, 16, 32, 128), BF16),
            pltpu.VMEM((16, 16, 32, 128), BF16),
            pltpu.VMEM((4, 512, 128), BF16),
            pltpu.VMEM((4, 16, 4, 32, 128), BF16),
            pltpu.VMEM((4, 16, 4, 32, 256), BF16),
            pltpu.VMEM((4, 512, 128), F32),
            pltpu.VMEM((4, 512, 128), BF16),
            pltpu.VMEM((4, 512, 128), BF16),
            pltpu.VMEM((64, 32, 128), BF16),
            pltpu.VMEM((32, 64, 128), BF16),
            pltpu.VMEM((2048, 128), F32),
            pltpu.VMEM((2048, 128), F32),
        ]
        + [dma((n,)) for n in (16, 16, 8, 8) * 2 + (8,) * 8 + (16, 16, 8, 8)],
        compiler_params=pltpu.CompilerParams(
            collective_id=0, has_side_effects=True, vmem_limit_bytes=56 * 2**20
        ),
    )(
        pair.reshape(2048, 128),
        gain_s.reshape(1, 128), project_s, gate_bias_s.reshape(1, 128), bias_s.T, out_s,
        gain_e.reshape(1, 128), project_e, gate_bias_e.reshape(1, 128), bias_e.T, out_e,
    )
    return out.reshape(pair.shape)


def solution(mesh):
    return jax.shard_map(
        local,
        mesh=mesh,
        in_specs=(P("row", "col", None), P(), P(), P(), P(), P(), P(), P(), P(), P(), P()),
        out_specs=P("row", "col", None),
        check_vma=False,
    )
```
